512 devices in a mesh: dp: 128 (over z, y, core), mp: 4 (over x).
Axes of the slice: x: 4, y: 4, z: 16, core: 2. Of those that a mesh axis runs over, the one named last changes fastest.
Arguments:
- hidden_in: bfloat16 [65536, 4096], P('dp', 'mp'), as said below
- grad_out: bfloat16 [65536, 4096], P('dp', 'mp'), may hold values from -3 to 3
- grad_qkv: bfloat16 [32768, 6144], P('dp', 'mp'), may hold values from -6 to 6
- qkv_weight: bfloat16 [4096, 6144], P('dp', 'mp'), may hold values from -0.09375 to 0.09375
- norm_gain: float32 [4096], P('mp'), may hold values from 0.1 to 1.9
- image_count: int32 [128], P('dp'), may hold values from 0 to 512, as said below
- image_pos: int32 [65536], P('dp'), may hold values from 0 to 512, as said below
- block_slot: int32 [128, 4], P('dp'), may hold values from -1 to 7, as said below
Outputs:
- grad_in: bfloat16 [65536, 4096], P('dp', 'mp')
The draws below stay inside these ranges and needn't reach their ends.
Inputs may be any that keep to these rules, and one draw needn't show every extreme that they name: `image_count`: each shard's count of image tokens; it is at most 512. `image_pos`: for shard i, its first image_count[i] entries are distinct increasing positions below 512; the remaining entries equal 512. `block_slot`: entry b of shard i is -1 exactly when b * 128 >= image_count[i]. Otherwise v // 2 < 4 and the block's cotangent lies in work slot v mod 2 of data index (i + v // 2) mod 128. No work slot is named twice; some data index has all 2 of its work slots named. Work slots that no block names hold rows of no token. `hidden_in`: activations of a real residual stream.
All inputs are finite; a program needn't handle non-finite values.
Results may differ from the reference program's by a relative error of at most 0.0095.
Values may be sent and summed in bfloat16 or wider, within the bound.
A program may use at most 64 MiB of HBM per device.

```python
import jax
import jax.numpy as jnp
from jax import lax

D = 4096
QKV = 6144
BLOCK_ROWS = 128
BLK = 4
REACH = 4
WORKB = 2
SEQ_DEV = 512
SHARDS = 128
GROUPS = 4
TOKENS = 65536
WORK_ROWS = 32768


def slot_layout(key):
    windows = SHARDS // 4
    keys = jax.random.split(key, 6)
    heavy_at = jax.random.randint(keys[0], (windows,), 0, 4)
    forced = jax.random.randint(keys[1], (), 0, windows)
    window_ids = jnp.arange(windows)
    heavy_at = jnp.where(window_ids == forced, 3, heavy_at)
    heavy_at = jnp.where(window_ids == (forced + 1) % windows, 0, heavy_at)
    heavy_dev = window_ids * 4 + heavy_at
    devices = jnp.arange(SHARDS)
    is_heavy = jnp.any(devices[:, None] == heavy_dev[None, :], axis=1)
    distance = (devices[:, None] - heavy_dev[None, :]) % SHARDS
    covered = jnp.sum(((distance >= 1) & (distance <= REACH - 1)).astype(jnp.int32), axis=1)
    coin_flip = jax.random.randint(keys[2], (SHARDS,), 0, 2)
    used_blocks = jnp.where(is_heavy, BLK, jnp.where(covered >= 2, 0, coin_flip))
    extra_rows = jax.random.randint(keys[3], (SHARDS,), 1, BLOCK_ROWS + 1)
    image_total = jnp.where(used_blocks > 0, (used_blocks - 1) * BLOCK_ROWS + extra_rows, 0)
    image_total = jnp.where(devices == heavy_dev[forced], BLK * BLOCK_ROWS, image_total)
    scores = jax.random.randint(keys[4], (SHARDS, BLK), 0, 1 << 20) * BLK + jnp.arange(BLK)[None, :]
    heavy_offsets = jnp.argsort(scores, axis=1)
    offsets = jnp.where(is_heavy[:, None], heavy_offsets, 0)
    columns = [(used_blocks >= 1).astype(jnp.int32)]
    for ahead in range(1, REACH):
        columns.append(is_heavy[(devices - ahead) % SHARDS].astype(jnp.int32))
    incoming = jnp.stack(columns, axis=1)
    rank_in = jnp.cumsum(incoming, axis=1) - incoming
    receiver = (devices[:, None] + offsets) % SHARDS
    slot_rank = rank_in[receiver, offsets]
    slot_code = offsets * WORKB + slot_rank
    block_ids = jnp.arange(BLK)[None, :]
    block_slot = jnp.where(block_ids < used_blocks[:, None], slot_code, -1)
    pos_scores = jax.random.randint(keys[5], (SHARDS, SEQ_DEV), 0, 1 << 20) * SEQ_DEV + jnp.arange(SEQ_DEV)[None, :]
    shuffled = jnp.argsort(pos_scores, axis=1)
    row_ids = jnp.arange(SEQ_DEV)[None, :]
    positions = jnp.sort(jnp.where(row_ids < image_total[:, None], shuffled, SEQ_DEV), axis=1)
    return (image_total.astype(jnp.int32), positions.reshape(-1).astype(jnp.int32), block_slot.astype(jnp.int32))


def draw_image_count(key, part):
    shared = slot_layout(key)
    return shared[0]


def draw_image_pos(key, part):
    shared = slot_layout(key)
    return shared[1]


def draw_block_slot(key, part):
    shared = slot_layout(key)
    return shared[2]


def draw_hidden_in(key, part):
    key = jax.random.fold_in(key, 7)
    keys = jax.random.split(key, 3)
    col_scale = 10.0 ** jax.random.uniform(keys[0], (D,), jnp.float32) / 4.0
    row_scale = 10.0 ** (jax.random.uniform(keys[1], (TOKENS, 1), jnp.float32) - 0.5)
    base = jax.random.normal(keys[2], (TOKENS, D), jnp.float32)
    return (base * col_scale[None, :] * row_scale).astype(jnp.bfloat16)


def shard_levels(stream_key, shape, shards, smallest, largest):
    loudness, own = 1.0, jax.random.fold_in(stream_key, 6)
    for position, shards_of in shards:
        steps = jnp.exp(jax.random.uniform(jax.random.fold_in(own, position), (shards_of,), jnp.float32, smallest / len(shards), largest / len(shards)))
        loudness = loudness * jnp.repeat(steps, shape[position] // shards_of).reshape([-1 if axis == position else 1 for axis in range(len(shape))])
    return loudness


def gaussian(own_key, extent, deviation, most, cuts=(), held_as=jnp.bfloat16):
    drawn = deviation * jax.random.normal(own_key, extent, jnp.float32)
    if cuts:
        drawn = drawn * shard_levels(own_key, extent, cuts, -0.22, 0.18)
    return jnp.clip(drawn, -most, most).astype(held_as)


def setup_inputs(seed: int = 0) -> dict:
    key_list = jax.random.split(jax.random.key(seed), 9)
    return {
        "hidden_in": draw_hidden_in(jax.random.fold_in(key_list[8], 71), 0),
        "grad_out": gaussian(key_list[1], (TOKENS, D), 0.5, 3.0, ((0, 128), (1, 4))),
        "grad_qkv": gaussian(key_list[2], (WORK_ROWS, QKV), 1.0, 6.0, ((0, 128), (1, 4))),
        "qkv_weight": gaussian(key_list[3], (D, QKV), D ** -0.5, 0.09375, ((0, 128), (1, 4))),
        "norm_gain": jnp.clip(1.0 + 0.18 * jax.random.normal(key_list[4], (D,), jnp.float32), 0.1, 1.9),
        "image_count": draw_image_count(jax.random.fold_in(key_list[8], 71), 0),
        "image_pos": draw_image_pos(jax.random.fold_in(key_list[8], 71), 0),
        "block_slot": draw_block_slot(jax.random.fold_in(key_list[8], 71), 0),
    }


def reference(hidden_in, grad_out, grad_qkv, qkv_weight, norm_gain, image_count, image_pos, block_slot):
    group_width = QKV // GROUPS

    def work_grads(cot_rows):
        summed = jnp.zeros((cot_rows.shape[0], D), jnp.float32)
        for column_group in range(GROUPS):
            low_col = column_group * group_width
            partial_value = jnp.dot(cot_rows[:, low_col:low_col + group_width], qkv_weight[:, low_col:low_col + group_width].T, preferred_element_type=jnp.float32)
            rounded = lax.optimization_barrier(partial_value.astype(jnp.bfloat16))
            summed = summed + rounded.astype(jnp.float32)
        return summed.astype(jnp.bfloat16)
    work_out = lax.map(work_grads, grad_qkv.reshape(SHARDS, WORKB * BLOCK_ROWS, QKV))
    block_out = work_out.reshape(SHARDS * WORKB, BLOCK_ROWS, D)

    def shard_grad(inputs):
        shard_index, x_in, out_in, image_total, positions, slot_code = inputs
        in_use = slot_code >= 0
        target = (shard_index + slot_code // WORKB) % SHARDS * WORKB + slot_code % WORKB
        target = jnp.where(in_use, target, 0).astype(jnp.int32)
        head_rows = block_out[target]
        head_rows = jnp.where(in_use[:, None, None], head_rows.astype(jnp.float32), 0.0)
        head_rows = head_rows.reshape(SEQ_DEV, D)
        row_index = jnp.arange(SEQ_DEV, dtype=jnp.int32)
        target_rows = jnp.where(row_index < image_total, positions, SEQ_DEV).astype(jnp.int32)
        head_grad = jnp.zeros((SEQ_DEV, D), jnp.float32).at[target_rows].add(head_rows, mode='drop')
        x_rows = x_in.astype(jnp.float32)
        scaled = head_grad * norm_gain[None, :]
        squares = lax.optimization_barrier(jnp.sum(x_rows * x_rows, axis=1, keepdims=True))
        cross_sum = lax.optimization_barrier(jnp.sum(scaled * x_rows, axis=1, keepdims=True))
        inv_rms = lax.rsqrt(squares / D + 1e-05)
        result = out_in.astype(jnp.float32) + inv_rms * scaled - x_rows * (inv_rms ** 3 * cross_sum / D)
        return result.astype(jnp.bfloat16)
    outputs = lax.map(shard_grad, (jnp.arange(SHARDS, dtype=jnp.int32), hidden_in.reshape(SHARDS, SEQ_DEV, D), grad_out.reshape(SHARDS, SEQ_DEV, D), image_count, image_pos.reshape(SHARDS, SEQ_DEV), block_slot))
    return outputs.reshape(TOKENS, D)
```

```python
import functools

import jax
import jax.numpy as jnp
from jax import lax
from jax.experimental import pallas as pl
from jax.experimental.pallas import tpu as pltpu
from jax.sharding import PartitionSpec as P

D = 4096
BLK = 4
REACH = 4
WORKB = 2
NY = 4
NC = 2
PLANE = NY * NC
MESH = pl.DeviceIdType.MESH
NT = (((1,), (1,)), ((), ()))


def kernel(
    nz, nx, slot_ref, c_ref, w_ref, tgt_ref, out_ref,
    cg, wg, ps, xr, sb, rb, rows, perm,
    c_send, c_recv, w_send, w_recv, x_send, x_recv, s_send, s_recv, own_sem,
):
    br = c_ref.shape[0] // WORKB
    wr = w_ref.shape[0]
    pn = ps.shape[3]
    me = lax.axis_index("dp")
    x = lax.axis_index("mp")
    z, lane = me // PLANE, lax.rem(me, PLANE)
    y, c = lane // NC, lax.rem(lane, NC)
    shards = nz * PLANE
    yp, ym, y2 = lax.rem(y + 1, NY), lax.rem(y + 3, NY), lax.rem(y + 2, NY)
    plane = z * PLANE
    sibling = plane + y * NC + 1 - c
    above, below = plane + yp * NC + c, plane + ym * NC + c
    z_up, z_down = lax.rem(me + PLANE, shards), lax.rem(me + shards - PLANE, shards)

    def remote(src, dst, send, recv, dp_to, x_to):
        return pltpu.make_async_remote_copy(
            src_ref=src, dst_ref=dst, send_sem=send, recv_sem=recv,
            device_id=(dp_to, x_to), device_id_type=MESH,
        )

    def landed(dst, recv):
        remote(dst, dst, own_sem.at[0], recv, sibling, x).wait_recv()

    barrier = pltpu.get_barrier_semaphore()

    def greet(dp_to, x_to):
        pl.semaphore_signal(barrier, inc=1, device_id=(dp_to, x_to), device_id_type=MESH)

    greet(z_up, x)
    greet(z_down, x)
    for r in range(1, PLANE):
        greet(plane + lax.rem(lane + r, PLANE), x)
    for r in range(1, nx):
        greet(me, lax.rem(x + r, nx))
    for r in range(1, REACH):
        greet(lax.rem(plane + shards - r, shards), x)

    @pl.when(lane >= PLANE - REACH + 1)
    def _():
        for r in range(PLANE):
            greet(lax.rem(plane + PLANE + r, shards), x)

    peers = 2 + (PLANE - 1) + (nx - 1) + (REACH - 1)
    pl.semaphore_wait(barrier, jnp.where(lane >= PLANE - REACH + 1, peers + PLANE, peers))

    pending = []

    def go(copy):
        copy.start()
        pending.append(copy)

    def slot_at(yy, cc, h):
        return cg.at[yy, pl.ds(pl.multiple_of((cc * WORKB + h) * br, 16), br)]

    def slot_sem(yy, cc, h):
        return c_recv.at[(yy * NC + cc) * WORKB + h]

    def own_half(h):
        return c_ref.at[pl.ds(h * br, br)]

    def w_at(zz):
        return wg.at[pl.ds(pl.multiple_of(zz * wr, 16), wr)]

    sends = 0
    for h, to in ((0, above), (1, below), (1, above), (0, below), (0, sibling), (1, sibling)):
        go(remote(own_half(h), slot_at(y, c, h), c_send.at[sends], slot_sem(y, c, h), to, x))
        sends += 1
    up_steps = nz // 2
    down_steps = nz - 1 - up_steps
    go(remote(w_ref, w_at(z), w_send.at[0], w_recv.at[z], z_up, x))
    go(remote(w_ref, w_at(z), w_send.at[nz], w_recv.at[z], z_down, x))
    own_c = pltpu.make_async_copy(c_ref, cg.at[y, pl.ds(pl.multiple_of(c * WORKB * br, 16), WORKB * br)], own_sem.at[0])
    own_w = pltpu.make_async_copy(w_ref, w_at(z), own_sem.at[1])
    own_c.start()
    own_w.start()

    width = perm.shape[0]
    src = lax.broadcasted_iota(jnp.int32, (width, 1), 0)
    goes_to = (lax.rem(src, pn) // wr) * (PLANE * wr) + (src // pn) * wr + lax.rem(src, wr)
    perm[...] = (goes_to == lax.broadcasted_iota(jnp.int32, (width, width), 1)).astype(jnp.float32).astype(jnp.bfloat16)
    own_c.wait()
    own_w.wait()

    def w_step(k):
        zz = lax.rem(z + nz - k, nz)
        landed(w_at(zz), w_recv.at[zz])
        if k < up_steps:
            go(remote(w_at(zz), w_at(zz), w_send.at[k], w_recv.at[zz], z_up, x))
        if k <= down_steps:
            zz = lax.rem(z + k, nz)
            landed(w_at(zz), w_recv.at[zz])
            if k < down_steps:
                go(remote(w_at(zz), w_at(zz), w_send.at[nz + k], w_recv.at[zz], z_down, x))

    def pass_on(yy, h, to=None):
        nonlocal sends
        landed(slot_at(yy, c, h), slot_sem(yy, c, h))
        for dest in ([] if to is None else [to]) + [sibling]:
            go(remote(slot_at(yy, c, h), slot_at(yy, c, h), c_send.at[sends], slot_sem(yy, c, h), dest, x))
            sends += 1

    def multiply(k, yy):
        for h in range(WORKB):
            landed(slot_at(yy, 1 - c, h), slot_sem(yy, 1 - c, h))

        @pl.loop(0, NC)
        def _(half):
            at = pl.ds(pl.multiple_of(half * WORKB * br, 16), WORKB * br)
            part = lax.dot_general(cg[yy, at], wg[...], NT, preferred_element_type=jnp.float32)
            part = part.astype(jnp.bfloat16)
            for xx in range(nx):
                ps[xx, yy, at] = part[:, xx * pn:(xx + 1) * pn]

        for r in range(1, nx):
            xx = lax.rem(x + r, nx)
            i = k * (nx - 1) + r - 1
            go(remote(ps.at[xx, yy], xr.at[r - 1, yy], x_send.at[i], x_recv.at[i], me, xx))

    def combine(k, yy):
        total = ps[x, yy].astype(jnp.float32)
        for r in range(1, nx):
            landed(xr.at[r - 1, yy], x_recv.at[k * (nx - 1) + r - 1])
            total = total + xr[r - 1, yy].astype(jnp.float32)
        total = total.astype(jnp.bfloat16)
        for s in range(NC * WORKB):
            sb[yy, s] = total[s * br:(s + 1) * br]
        for cc in range(NC):
            for o in range(REACH):
                dest = dest_of(yy, cc, o)

                @pl.when(dest == me)
                def _():
                    pltpu.make_async_copy(*route(yy, cc, o)).start()

                @pl.when(dest != me)
                def _():
                    deliver(k, yy, cc, o).start()

    def dest_of(yy, cc, o):
        return lax.rem(plane + yy * NC + cc - o + shards, shards)

    def route(yy, cc, o):
        from_ref = sb.at[yy, pl.ds(cc * WORKB, WORKB)]
        return from_ref, rb.at[lane, pl.ds(o * WORKB, WORKB)], s_recv.at[lane * REACH + o]

    def deliver(k, yy, cc, o):
        from_ref, to_ref, recv = route(yy, cc, o)
        return remote(from_ref, to_ref, s_send.at[(k * NC + cc) * REACH + o], recv, dest_of(yy, cc, o), x)

    order = [y, ym, yp, y2]
    for k in range(1, up_steps + 1):
        w_step(k)
        if k == up_steps // 2:
            pass_on(ym, 0, above)
            pass_on(yp, 1, below)
    multiply(0, order[0])
    pass_on(ym, 1)
    pass_on(yp, 0)
    multiply(1, order[1])
    multiply(2, order[2])
    combine(0, order[0])
    pass_on(y2, 0)
    pass_on(y2, 1)
    combine(1, order[1])
    multiply(3, order[3])
    combine(2, order[2])
    combine(3, order[3])

    for s in range(PLANE):
        for o in range(REACH):
            landed(rb.at[s, pl.ds(o * WORKB, WORKB)], s_recv.at[s * REACH + o])
    for b in range(BLK):
        v = slot_ref[0, b]
        used = v >= 0
        pick = jnp.maximum(v, 0)
        for s in range(PLANE):
            block = rb[s, pick]
            rows[b * br:(b + 1) * br, s * pn:(s + 1) * pn] = jnp.where(used, block, jnp.zeros_like(block))
    seq = BLK * br
    place = (lax.broadcasted_iota(jnp.int32, (seq, seq), 0) == tgt_ref[...]).astype(jnp.float32).astype(jnp.bfloat16)
    placed = jnp.dot(place, rows[...], preferred_element_type=jnp.float32).astype(jnp.bfloat16)
    out_ref[...] = jnp.dot(placed, perm[...], preferred_element_type=jnp.float32).astype(jnp.bfloat16)

    for copy in pending:
        copy.wait_send()
    for k in range(NY):
        for cc in range(NC):
            for o in range(REACH):
                @pl.when(dest_of(order[k], cc, o) != me)
                def _():
                    deliver(k, order[k], cc, o).wait_send()


def shards(nz, nx, hidden_in, grad_out, grad_qkv, qkv_weight, norm_gain, image_count, image_pos, block_slot):
    seq, cols = hidden_in.shape
    br = seq // BLK
    depth = grad_qkv.shape[1]
    wr = qkv_weight.shape[0]
    pn = nz * wr // nx
    row_index = jnp.arange(seq, dtype=jnp.int32)
    target = jnp.where(row_index < image_count[0], image_pos, seq)[None, :]
    bf16 = jnp.bfloat16
    dma = pltpu.SemaphoreType.DMA
    vmem = pl.BlockSpec(memory_space=pltpu.VMEM)
    head_grad = pl.pallas_call(
        functools.partial(kernel, nz, nx),
        out_shape=jax.ShapeDtypeStruct((seq, cols), bf16),
        in_specs=[pl.BlockSpec(memory_space=pltpu.SMEM), vmem, vmem, vmem],
        out_specs=vmem,
        scratch_shapes=[
            pltpu.VMEM((NY, NC * WORKB * br, depth), bf16),
            pltpu.VMEM((nz * wr, depth), bf16),
            pltpu.VMEM((nx, NY, NC * WORKB * br, pn), bf16),
            pltpu.VMEM((nx - 1, NY, NC * WORKB * br, pn), bf16),
            pltpu.VMEM((NY, NC * WORKB, br, pn), bf16),
            pltpu.VMEM((PLANE, REACH * WORKB, br, pn), bf16),
            pltpu.VMEM((seq, cols), bf16),
            pltpu.VMEM((cols, cols), bf16),
            dma((14,)),
            dma((PLANE * WORKB,)),
            dma((2 * nz,)),
            dma((nz,)),
            dma((NY * (nx - 1),)),
            dma((NY * (nx - 1),)),
            dma((PLANE * REACH,)),
            dma((PLANE * REACH,)),
            dma((2,)),
        ],
        compiler_params=pltpu.CompilerParams(
            collective_id=0, has_side_effects=True, vmem_limit_bytes=44 * 1024 * 1024
        ),
    )(block_slot, grad_qkv, qkv_weight, target)

    x_rows = hidden_in.astype(jnp.float32)
    scaled = head_grad.astype(jnp.float32) * norm_gain[None, :]
    local = jnp.stack([jnp.sum(x_rows * x_rows, axis=1), jnp.sum(scaled * x_rows, axis=1)])
    squares, cross = lax.psum(local, "mp")
    inv_rms = lax.rsqrt(squares / D + 1e-05)
    result = (
        grad_out.astype(jnp.float32)
        + inv_rms[:, None] * scaled
        - x_rows * (inv_rms**3 * cross / D)[:, None]
    )
    return result.astype(bf16)


def solution(mesh):
    nz, nx = mesh.shape["dp"] // PLANE, mesh.shape["mp"]
    return jax.shard_map(
        functools.partial(shards, nz, nx),
        mesh=mesh,
        in_specs=(
            P("dp", "mp"),
            P("dp", "mp"),
            P("dp", "mp"),
            P("dp", "mp"),
            P("mp"),
            P("dp"),
            P("dp"),
            P("dp", None),
        ),
        out_specs=P("dp", "mp"),
        check_vma=False,
    )
```

```python
import functools

import jax
import jax.numpy as jnp
from jax import lax
from jax.experimental import pallas as pl
from jax.experimental.pallas import tpu as pltpu
from jax.sharding import PartitionSpec as P

D = 4096
BLK = 4
REACH = 4
WORKB = 2
NY = 4
NC = 2
PLANE = NY * NC
WCUT = 2
MESH = pl.DeviceIdType.MESH
NT = (((1,), (1,)), ((), ()))


def kernel(
    nz, nx, slot_ref, count_ref, pos_ref, gain_ref, hid_ref, c_ref, w_ref, grad_ref, stat_ref,
    cg, wg, ps, xr, sb, rb, rt, hid, stats,
    c_send, c_recv, w_send, w_recv, x_send, x_recv, s_send, s_recv, t_send, t_recv, own_sem,
):
    br = c_ref.shape[0] // WORKB
    wr, depth = w_ref.shape
    pn = ps.shape[2]
    me = lax.axis_index("dp")
    x = lax.axis_index("mp")
    z, lane = me // PLANE, lax.rem(me, PLANE)
    y, c = lane // NC, lax.rem(lane, NC)
    shards = nz * PLANE
    yp, ym, y2 = lax.rem(y + 1, NY), lax.rem(y + 3, NY), lax.rem(y + 2, NY)
    plane = z * PLANE
    sibling = plane + y * NC + 1 - c
    above, below = plane + yp * NC + c, plane + ym * NC + c
    z_up, z_down = lax.rem(me + PLANE, shards), lax.rem(me + shards - PLANE, shards)

    def remote(src, dst, send, recv, dp_to, x_to):
        return pltpu.make_async_remote_copy(
            src_ref=src, dst_ref=dst, send_sem=send, recv_sem=recv,
            device_id=(dp_to, x_to), device_id_type=MESH,
        )

    def landed(dst, recv):
        remote(dst, dst, own_sem.at[0], recv, sibling, x).wait_recv()

    barrier = pltpu.get_barrier_semaphore()

    def greet(dp_to, x_to):
        pl.semaphore_signal(barrier, inc=1, device_id=(dp_to, x_to), device_id_type=MESH)

    greet(z_up, x)
    greet(z_down, x)
    for r in range(1, PLANE):
        greet(plane + lax.rem(lane + r, PLANE), x)
    for r in range(1, nx):
        greet(me, lax.rem(x + r, nx))
    for r in range(1, REACH):
        greet(lax.rem(plane + shards - r, shards), x)

    @pl.when(lane >= PLANE - REACH + 1)
    def _():
        for r in range(PLANE):
            greet(lax.rem(plane + PLANE + r, shards), x)

    def w_part(ref, base, p):
        at = base + (p // WCUT) * (wr // WCUT)
        return ref.at[pl.ds(pl.multiple_of(at, 16), wr // WCUT), pl.ds((p % WCUT) * (depth // WCUT), depth // WCUT)]

    own_c = pltpu.make_async_copy(c_ref, cg.at[y, pl.ds(pl.multiple_of(c * WORKB * br, 16), WORKB * br)], own_sem.at[0])
    own_w = pltpu.make_async_copy(w_ref, wg.at[pl.ds(pl.multiple_of(z * wr, 16), wr)], own_sem.at[1])
    own_h = pltpu.make_async_copy(hid_ref, hid, own_sem.at[2])
    own_c.start()
    own_w.start()
    own_h.start()
    peers = 2 + (PLANE - 1) + (nx - 1) + (REACH - 1)
    pl.semaphore_wait(barrier, jnp.where(lane >= PLANE - REACH + 1, peers + PLANE, peers))

    pending = []

    def go(copy):
        copy.start()
        pending.append(copy)

    def slot_at(yy, cc, h):
        return cg.at[yy, pl.ds(pl.multiple_of((cc * WORKB + h) * br, 16), br)]

    def slot_sem(yy, cc, h):
        return c_recv.at[(yy * NC + cc) * WORKB + h]

    def own_half(h):
        return c_ref.at[pl.ds(h * br, br)]

    parts = WCUT * WCUT
    up_steps = nz // 2
    down_steps = nz - 1 - up_steps

    def w_go(src, zz, p, k, up):
        send = w_send.at[((0 if up else nz) + k) * parts + p]
        go(remote(src, w_part(wg, zz * wr, p), send, w_recv.at[zz * parts + p], z_up if up else z_down, x))

    sends = 0
    for p in range(parts):
        w_go(w_part(w_ref, 0, p), z, p, 0, True)
        w_go(w_part(w_ref, 0, p), z, p, 0, False)
    for h, to in ((0, above), (1, below), (1, above), (0, below), (0, sibling), (1, sibling)):
        go(remote(own_half(h), slot_at(y, c, h), c_send.at[sends], slot_sem(y, c, h), to, x))
        sends += 1

    def row_sums(value):
        lanes = value[:, :128]
        for t in range(1, value.shape[1] // 128):
            lanes = lanes + value[:, t * 128:(t + 1) * 128]
        return jnp.sum(lanes.T, axis=0, keepdims=True)

    own_c.wait()
    own_w.wait()
    own_h.wait()
    h_rows = hid[...].astype(jnp.float32)
    stats[0] = jnp.zeros(stats.shape[1:], jnp.float32)
    stats[0, 0:1, :] = row_sums(h_rows * h_rows)

    def w_step(k):
        for p in range(parts):
            zz = lax.rem(z + nz - k, nz)
            landed(w_part(wg, zz * wr, p), w_recv.at[zz * parts + p])
            if k < up_steps:
                w_go(w_part(wg, zz * wr, p), zz, p, k, True)
            if k <= down_steps:
                zz = lax.rem(z + k, nz)
                landed(w_part(wg, zz * wr, p), w_recv.at[zz * parts + p])
                if k < down_steps:
                    w_go(w_part(wg, zz * wr, p), zz, p, k, False)

    def pass_on(yy, h, to=None):
        nonlocal sends
        landed(slot_at(yy, c, h), slot_sem(yy, c, h))
        for dest in ([] if to is None else [to]) + [sibling]:
            go(remote(slot_at(yy, c, h), slot_at(yy, c, h), c_send.at[sends], slot_sem(yy, c, h), dest, x))
            sends += 1

    def multiply(k, yy):
        for h in range(WORKB):
            landed(slot_at(yy, 1 - c, h), slot_sem(yy, 1 - c, h))

        @pl.loop(0, nx)
        def _(xx):
            at = pl.ds(pl.multiple_of(xx * pn, 16), pn)
            part = lax.dot_general(wg[at], cg[yy], NT, preferred_element_type=jnp.float32)
            ps[xx, yy] = part.astype(jnp.bfloat16)

        for r in range(1, nx):
            xx = lax.rem(x + r, nx)
            i = k * (nx - 1) + r - 1
            go(remote(ps.at[xx, yy], xr.at[r - 1, yy], x_send.at[i], x_recv.at[i], me, xx))

    def combine(k, yy):
        total = ps[x, yy].astype(jnp.float32)
        for r in range(1, nx):
            landed(xr.at[r - 1, yy], x_recv.at[k * (nx - 1) + r - 1])
            total = total + xr[r - 1, yy].astype(jnp.float32)
        total = total.astype(jnp.bfloat16)
        for s in range(NC * WORKB):
            sb[yy, s] = total[:, s * br:(s + 1) * br].reshape(sb.shape[2:])
        for cc in range(NC):
            for o in range(REACH):
                dest = dest_of(yy, cc, o)

                @pl.when(dest == me)
                def _():
                    pltpu.make_async_copy(*route(yy, cc, o)).start()

                @pl.when(dest != me)
                def _():
                    deliver(k, yy, cc, o).start()

    def dest_of(yy, cc, o):
        return lax.rem(plane + yy * NC + cc - o + shards, shards)

    def candidates(o, source):
        return rb.at[pl.ds(o * WORKB, WORKB), :, source]

    def route(yy, cc, o):
        from_ref = sb.at[yy, pl.ds(cc * WORKB, WORKB)]
        return from_ref, candidates(o, lane), s_recv.at[lane * REACH + o]

    def deliver(k, yy, cc, o):
        from_ref, to_ref, recv = route(yy, cc, o)
        return remote(from_ref, to_ref, s_send.at[(k * NC + cc) * REACH + o], recv, dest_of(yy, cc, o), x)

    order = [y, ym, yp, y2]
    for k in range(1, up_steps + 1):
        w_step(k)
        if k == up_steps // 2:
            pass_on(ym, 0, above)
            pass_on(yp, 1, below)
        if k == up_steps - 1:
            pass_on(ym, 1)
            pass_on(yp, 0)
    for k in range(3):
        multiply(k, order[k])
    pass_on(y2, 0)
    pass_on(y2, 1)
    combine(0, order[0])
    multiply(3, order[3])
    for k in range(1, 4):
        combine(k, order[k])

    seq = BLK * br
    target = jnp.where(lax.broadcasted_iota(jnp.int32, (1, seq), 1) < count_ref[0], pos_ref[...], seq)
    place = (lax.broadcasted_iota(jnp.int32, (seq, seq), 0) == target).astype(jnp.float32).astype(jnp.bfloat16)
    for s in range(PLANE):
        for o in range(REACH):
            landed(candidates(o, s), s_recv.at[s * REACH + o])
    for b in range(BLK):
        v = slot_ref[0, b]
        block = rb[jnp.maximum(v, 0)].reshape(rt.shape[0], br)
        rt[:, b * br:(b + 1) * br] = jnp.where(v >= 0, block, jnp.zeros_like(block))
    placed = lax.dot_general(place, rt[...], NT, preferred_element_type=jnp.float32)
    grad_ref[...] = placed.astype(jnp.bfloat16)
    stats[0, 1:2, :] = row_sums(placed * gain_ref[...] * hid[...].astype(jnp.float32))
    for r in range(1, nx):
        go(remote(stats.at[0], stats.at[r], t_send.at[r - 1], t_recv.at[r - 1], me, lax.rem(x + r, nx)))
    total = stats[0]
    for r in range(1, nx):
        landed(stats.at[r], t_recv.at[r - 1])
        total = total + stats[r]
    stat_ref[...] = total

    for copy in pending:
        copy.wait_send()
    for k in range(NY):
        for cc in range(NC):
            for o in range(REACH):
                @pl.when(dest_of(order[k], cc, o) != me)
                def _():
                    deliver(k, order[k], cc, o).wait_send()


def shards(nz, nx, hidden_in, grad_out, grad_qkv, qkv_weight, norm_gain, image_count, image_pos, block_slot):
    seq, cols = hidden_in.shape
    br = seq // BLK
    depth = grad_qkv.shape[1]
    wr = qkv_weight.shape[0]
    pn = nz * wr // nx
    bf16 = jnp.bfloat16
    dma = pltpu.SemaphoreType.DMA
    vmem = pl.BlockSpec(memory_space=pltpu.VMEM)
    smem = pl.BlockSpec(memory_space=pltpu.SMEM)
    hbm = pl.BlockSpec(memory_space=pl.ANY)
    chip_rows = NC * WORKB * br
    parts = WCUT * WCUT
    head_grad, stats = pl.pallas_call(
        functools.partial(kernel, nz, nx),
        out_shape=(jax.ShapeDtypeStruct((seq, cols), bf16), jax.ShapeDtypeStruct((8, seq), jnp.float32)),
        in_specs=[smem, smem, vmem, vmem, hbm, hbm, hbm],
        out_specs=(vmem, vmem),
        scratch_shapes=[
            pltpu.VMEM((NY, chip_rows, depth), bf16),
            pltpu.VMEM((nz * wr, depth), bf16),
            pltpu.VMEM((nx, NY, pn, chip_rows), bf16),
            pltpu.VMEM((nx - 1, NY, pn, chip_rows), bf16),
            pltpu.VMEM((NY, NC * WORKB, nz // nx, wr, br), bf16),
            pltpu.VMEM((REACH * WORKB, nz // nx, PLANE, wr, br), bf16),
            pltpu.VMEM((cols, seq), bf16),
            pltpu.VMEM((seq, cols), bf16),
            pltpu.VMEM((nx, 8, seq), jnp.float32),
            dma((14,)),
            dma((PLANE * WORKB,)),
            dma((2 * nz * parts,)),
            dma((nz * parts,)),
            dma((NY * (nx - 1),)),
            dma((NY * (nx - 1),)),
            dma((PLANE * REACH,)),
            dma((PLANE * REACH,)),
            dma((nx - 1,)),
            dma((nx - 1,)),
            dma((3,)),
        ],
        compiler_params=pltpu.CompilerParams(
            collective_id=0, has_side_effects=True, vmem_limit_bytes=60 * 1024 * 1024
        ),
    )(block_slot, image_count, image_pos[None, :], norm_gain[None, :], hidden_in, grad_qkv, qkv_weight)

    squares, cross = stats[0], stats[1]
    inv_rms = lax.rsqrt(squares / D + 1e-05)
    result = (
        grad_out.astype(jnp.float32)
        + inv_rms[:, None] * (head_grad.astype(jnp.float32) * norm_gain[None, :])
        - hidden_in.astype(jnp.float32) * (inv_rms**3 * cross / D)[:, None]
    )
    return result.astype(bf16)


def solution(mesh):
    nz, nx = mesh.shape["dp"] // PLANE, mesh.shape["mp"]
    return jax.shard_map(
        functools.partial(shards, nz, nx),
        mesh=mesh,
        in_specs=(
            P("dp", "mp"),
            P("dp", "mp"),
            P("dp", "mp"),
            P("dp", "mp"),
            P("mp"),
            P("dp"),
            P("dp"),
            P("dp", None),
        ),
        out_specs=P("dp", "mp"),
        check_vma=False,
    )
```

```python
import functools

import jax
import jax.numpy as jnp
from jax import lax
from jax.experimental import pallas as pl
from jax.experimental.pallas import tpu as pltpu
from jax.sharding import PartitionSpec as P

D = 4096
BLK = 4
REACH = 4
WORKB = 2
NY = 4
NC = 2
PLANE = NY * NC
W_ROW_CUT = 2
W_COL_CUT = 1
MESH = pl.DeviceIdType.MESH
NT = (((1,), (1,)), ((), ()))


def kernel(
    nz, nx, slot_ref, count_ref, pos_ref, gain_ref, hid_ref, c_ref, w_ref, grad_ref, stat_ref,
    cg, wg, ps, xr, sb, rb, rt, hid, stats,
    c_send, c_recv, w_send, w_recv, x_send, x_recv, s_send, s_recv, t_send, t_recv, own_sem,
):
    br = c_ref.shape[0] // WORKB
    wr, depth = w_ref.shape
    pn = ps.shape[2]
    me = lax.axis_index("dp")
    x = lax.axis_index("mp")
    z, lane = me // PLANE, lax.rem(me, PLANE)
    y, c = lane // NC, lax.rem(lane, NC)
    shards = nz * PLANE
    yp, ym, y2 = lax.rem(y + 1, NY), lax.rem(y + 3, NY), lax.rem(y + 2, NY)
    plane = z * PLANE
    sibling = plane + y * NC + 1 - c
    above, below = plane + yp * NC + c, plane + ym * NC + c
    z_up, z_down = lax.rem(me + PLANE, shards), lax.rem(me + shards - PLANE, shards)

    def remote(src, dst, send, recv, dp_to, x_to):
        return pltpu.make_async_remote_copy(
            src_ref=src, dst_ref=dst, send_sem=send, recv_sem=recv,
            device_id=(dp_to, x_to), device_id_type=MESH,
        )

    def landed(dst, recv):
        remote(dst, dst, own_sem.at[0], recv, sibling, x).wait_recv()

    barrier = pltpu.get_barrier_semaphore()

    def greet(dp_to, x_to):
        pl.semaphore_signal(barrier, inc=1, device_id=(dp_to, x_to), device_id_type=MESH)

    greet(z_up, x)
    greet(z_down, x)
    for r in range(1, PLANE):
        greet(plane + lax.rem(lane + r, PLANE), x)
    for r in range(1, nx):
        greet(me, lax.rem(x + r, nx))

    def w_part(ref, base, p):
        tall, wide = wr // W_ROW_CUT, depth // W_COL_CUT
        at = base + (p // W_COL_CUT) * tall
        return ref.at[pl.ds(pl.multiple_of(at, 16), tall), pl.ds((p % W_COL_CUT) * wide, wide)]

    own_c = pltpu.make_async_copy(c_ref, cg.at[y, pl.ds(pl.multiple_of(c * WORKB * br, 16), WORKB * br)], own_sem.at[0])
    own_w = pltpu.make_async_copy(w_ref, wg.at[pl.ds(pl.multiple_of(z * wr, 16), wr)], own_sem.at[1])
    own_h = pltpu.make_async_copy(hid_ref, hid, own_sem.at[2])
    own_c.start()
    own_w.start()
    own_h.start()
    pl.semaphore_wait(barrier, 2 + (PLANE - 1) + (nx - 1))

    pending = []

    def go(copy):
        copy.start()
        pending.append(copy)

    def slot_at(yy, cc, h):
        return cg.at[yy, pl.ds(pl.multiple_of((cc * WORKB + h) * br, 16), br)]

    def slot_sem(yy, cc, h):
        return c_recv.at[(yy * NC + cc) * WORKB + h]

    def own_half(h):
        return c_ref.at[pl.ds(h * br, br)]

    parts = W_ROW_CUT * W_COL_CUT
    up_steps = nz // 2
    down_steps = nz - 1 - up_steps

    def w_go(src, zz, p, k, up):
        send = w_send.at[((0 if up else nz) + k) * parts + p]
        go(remote(src, w_part(wg, zz * wr, p), send, w_recv.at[zz * parts + p], z_up if up else z_down, x))

    sends = 0
    for p in range(parts):
        w_go(w_part(w_ref, 0, p), z, p, 0, True)
        w_go(w_part(w_ref, 0, p), z, p, 0, False)
    for h, to in ((0, above), (1, below), (1, above), (0, below), (0, sibling), (1, sibling)):
        go(remote(own_half(h), slot_at(y, c, h), c_send.at[sends], slot_sem(y, c, h), to, x))
        sends += 1

    def row_sums(value):
        lanes = value[:, :128]
        for t in range(1, value.shape[1] // 128):
            lanes = lanes + value[:, t * 128:(t + 1) * 128]
        return jnp.sum(lanes.T, axis=0, keepdims=True)

    own_c.wait()
    own_w.wait()
    own_h.wait()
    h_rows = hid[...].astype(jnp.float32)
    stats[0] = jnp.zeros(stats.shape[1:], jnp.float32)
    stats[0, 0:1, :] = row_sums(h_rows * h_rows)

    def w_step(k):
        for p in range(parts):
            zz = lax.rem(z + nz - k, nz)
            landed(w_part(wg, zz * wr, p), w_recv.at[zz * parts + p])
            if k < up_steps:
                w_go(w_part(wg, zz * wr, p), zz, p, k, True)
            if k <= down_steps:
                zz = lax.rem(z + k, nz)
                landed(w_part(wg, zz * wr, p), w_recv.at[zz * parts + p])
                if k < down_steps:
                    w_go(w_part(wg, zz * wr, p), zz, p, k, False)

    def pass_on(yy, h, to=None):
        nonlocal sends
        landed(slot_at(yy, c, h), slot_sem(yy, c, h))
        for dest in ([] if to is None else [to]) + [sibling]:
            go(remote(slot_at(yy, c, h), slot_at(yy, c, h), c_send.at[sends], slot_sem(yy, c, h), dest, x))
            sends += 1

    def multiply(k, yy):
        for h in range(WORKB):
            landed(slot_at(yy, 1 - c, h), slot_sem(yy, 1 - c, h))

        part = lax.dot_general(wg[...], cg[yy], NT, preferred_element_type=jnp.float32).astype(jnp.bfloat16)
        for xx in range(nx):
            ps[xx, yy] = part[xx * pn:(xx + 1) * pn]

        for r in range(1, nx):
            xx = lax.rem(x + r, nx)
            i = k * (nx - 1) + r - 1
            go(remote(ps.at[xx, yy], xr.at[r - 1, yy], x_send.at[i], x_recv.at[i], me, xx))

    def combine(k, yy):
        total = ps[x, yy].astype(jnp.float32)
        for r in range(1, nx):
            landed(xr.at[r - 1, yy], x_recv.at[k * (nx - 1) + r - 1])
            total = total + xr[r - 1, yy].astype(jnp.float32)
        total = total.astype(jnp.bfloat16)
        for s in range(NC * WORKB):
            sb[yy, s] = total[:, s * br:(s + 1) * br].reshape(sb.shape[2:])
        for cc in range(NC):
            for o in range(REACH):
                dest = dest_of(yy, cc, o)

                @pl.when(dest == me)
                def _():
                    pltpu.make_async_copy(*route(yy, cc, o)).start()

                @pl.when(dest != me)
                def _():
                    deliver(k, yy, cc, o).start()

    def dest_of(yy, cc, o):
        return lax.rem(plane + yy * NC + cc - o + shards, shards)

    def candidates(o, source):
        return rb.at[pl.ds(o * WORKB, WORKB), :, source]

    def route(yy, cc, o):
        from_ref = sb.at[yy, pl.ds(cc * WORKB, WORKB)]
        return from_ref, candidates(o, lane), s_recv.at[lane * REACH + o]

    def deliver(k, yy, cc, o):
        from_ref, to_ref, recv = route(yy, cc, o)
        return remote(from_ref, to_ref, s_send.at[(k * NC + cc) * REACH + o], recv, dest_of(yy, cc, o), x)

    order = [ym, y2, y, yp]
    for k in range(1, up_steps + 1):
        w_step(k)
        if k == up_steps // 2:
            pass_on(ym, 0, above)
            pass_on(yp, 1, below)
        if k == up_steps - 1:
            pass_on(ym, 1)
            pass_on(yp, 0)
    multiply(0, order[0])
    pass_on(y2, 0)
    pass_on(y2, 1)
    multiply(1, order[1])
    multiply(2, order[2])
    combine(0, order[0])
    multiply(3, order[3])
    for k in range(1, NY):
        combine(k, order[k])

    seq = BLK * br
    target = jnp.where(lax.broadcasted_iota(jnp.int32, (1, seq), 1) < count_ref[0], pos_ref[...], seq)
    place = (lax.broadcasted_iota(jnp.int32, (seq, seq), 0) == target).astype(jnp.float32).astype(jnp.bfloat16)
    for s in range(PLANE):
        for o in range(REACH):
            landed(candidates(o, s), s_recv.at[s * REACH + o])
    for b in range(BLK):
        v = slot_ref[0, b]
        block = rb[jnp.maximum(v, 0)].reshape(rt.shape[0], br)
        rt[:, b * br:(b + 1) * br] = jnp.where(v >= 0, block, jnp.zeros_like(block))
    placed = lax.dot_general(place, rt[...], NT, preferred_element_type=jnp.float32)
    grad_ref[...] = placed.astype(jnp.bfloat16)
    stats[0, 1:2, :] = row_sums(placed * gain_ref[...] * hid[...].astype(jnp.float32))
    for r in range(1, nx):
        go(remote(stats.at[0], stats.at[r], t_send.at[r - 1], t_recv.at[r - 1], me, lax.rem(x + r, nx)))
    total = stats[0]
    for r in range(1, nx):
        landed(stats.at[r], t_recv.at[r - 1])
        total = total + stats[r]
    stat_ref[...] = total

    for copy in pending:
        copy.wait_send()
    for k in range(NY):
        for cc in range(NC):
            for o in range(REACH):
                @pl.when(dest_of(order[k], cc, o) != me)
                def _():
                    deliver(k, order[k], cc, o).wait_send()


def shards(nz, nx, hidden_in, grad_out, grad_qkv, qkv_weight, norm_gain, image_count, image_pos, block_slot):
    seq, cols = hidden_in.shape
    br = seq // BLK
    depth = grad_qkv.shape[1]
    wr = qkv_weight.shape[0]
    pn = nz * wr // nx
    bf16 = jnp.bfloat16
    dma = pltpu.SemaphoreType.DMA
    vmem = pl.BlockSpec(memory_space=pltpu.VMEM)
    smem = pl.BlockSpec(memory_space=pltpu.SMEM)
    hbm = pl.BlockSpec(memory_space=pl.ANY)
    chip_rows = NC * WORKB * br
    parts = W_ROW_CUT * W_COL_CUT
    head_grad, stats = pl.pallas_call(
        functools.partial(kernel, nz, nx),
        out_shape=(jax.ShapeDtypeStruct((seq, cols), bf16), jax.ShapeDtypeStruct((8, seq), jnp.float32)),
        in_specs=[smem, smem, vmem, vmem, hbm, hbm, hbm],
        out_specs=(vmem, vmem),
        scratch_shapes=[
            pltpu.VMEM((NY, chip_rows, depth), bf16),
            pltpu.VMEM((nz * wr, depth), bf16),
            pltpu.VMEM((nx, NY, pn, chip_rows), bf16),
            pltpu.VMEM((nx - 1, NY, pn, chip_rows), bf16),
            pltpu.VMEM((NY, NC * WORKB, nz // nx, wr, br), bf16),
            pltpu.VMEM((REACH * WORKB, nz // nx, PLANE, wr, br), bf16),
            pltpu.VMEM((cols, seq), bf16),
            pltpu.VMEM((seq, cols), bf16),
            pltpu.VMEM((nx, 8, seq), jnp.float32),
            dma((14,)),
            dma((PLANE * WORKB,)),
            dma((2 * nz * parts,)),
            dma((nz * parts,)),
            dma((NY * (nx - 1),)),
            dma((NY * (nx - 1),)),
            dma((PLANE * REACH,)),
            dma((PLANE * REACH,)),
            dma((nx - 1,)),
            dma((nx - 1,)),
            dma((3,)),
        ],
        compiler_params=pltpu.CompilerParams(
            collective_id=0, has_side_effects=True, vmem_limit_bytes=60 * 1024 * 1024
        ),
    )(block_slot, image_count, image_pos[None, :], norm_gain[None, :], hidden_in, grad_qkv, qkv_weight)

    squares, cross = stats[0], stats[1]
    inv_rms = lax.rsqrt(squares / D + 1e-05)
    result = (
        grad_out.astype(jnp.float32)
        + inv_rms[:, None] * (head_grad.astype(jnp.float32) * norm_gain[None, :])
        - hidden_in.astype(jnp.float32) * (inv_rms**3 * cross / D)[:, None]
    )
    return result.astype(bf16)


def solution(mesh):
    nz, nx = mesh.shape["dp"] // PLANE, mesh.shape["mp"]
    return jax.shard_map(
        functools.partial(shards, nz, nx),
        mesh=mesh,
        in_specs=(
            P("dp", "mp"),
            P("dp", "mp"),
            P("dp", "mp"),
            P("dp", "mp"),
            P("mp"),
            P("dp"),
            P("dp"),
            P("dp", None),
        ),
        out_specs=P("dp", "mp"),
        check_vma=False,
    )
```

```python
import functools

import jax
import jax.numpy as jnp
from jax import lax
from jax.experimental import pallas as pl
from jax.experimental.pallas import tpu as pltpu
from jax.sharding import PartitionSpec as P

D = 4096
BLK = 4
REACH = 4
WORKB = 2
NY = 4
NC = 2
PLANE = NY * NC
REACHED = (REACH + NC - 1 + NC - 1) // NC
SLOTS = (REACH + NC - 1) * WORKB
STAGES = (-1, 2, 0, 1)
W_ROW_CUT = 2
W_COL_CUT = 1
MESH = pl.DeviceIdType.MESH
NT = (((1,), (1,)), ((), ()))


def kernel(
    nz, nx, slot_ref, count_ref, pos_ref, gain_ref, hid_ref, c_ref, w_ref, grad_ref, stat_ref,
    cg, wg, ps, xr, sb, rb, rt, hid, stats,
    c_send, c_recv, w_send, w_recv, x_send, x_recv, s_send, s_recv, t_send, t_recv, own_sem,
):
    br = c_ref.shape[0] // WORKB
    wr, depth = w_ref.shape
    pn = ps.shape[2]
    me = lax.axis_index("dp")
    x = lax.axis_index("mp")
    z, lane = me // PLANE, lax.rem(me, PLANE)
    y, c = lane // NC, lax.rem(lane, NC)
    shards = nz * PLANE
    yp, ym, y2 = lax.rem(y + 1, NY), lax.rem(y + 3, NY), lax.rem(y + 2, NY)
    plane = z * PLANE
    xp, xl, x2 = lax.rem(x + 1, nx), lax.rem(x + nx - 1, nx), lax.rem(x + 2, nx)
    sibling = plane + y * NC + 1 - c
    above, below = plane + yp * NC + c, plane + ym * NC + c
    z_up, z_down = lax.rem(me + PLANE, shards), lax.rem(me + shards - PLANE, shards)

    def remote(src, dst, send, recv, dp_to, x_to):
        return pltpu.make_async_remote_copy(
            src_ref=src, dst_ref=dst, send_sem=send, recv_sem=recv,
            device_id=(dp_to, x_to), device_id_type=MESH,
        )

    def landed(dst, recv):
        remote(dst, dst, own_sem.at[0], recv, sibling, x).wait_recv()

    barrier = pltpu.get_barrier_semaphore()

    def greet(dp_to, x_to):
        pl.semaphore_signal(barrier, inc=1, device_id=(dp_to, x_to), device_id_type=MESH)

    greet(z_up, x)
    greet(z_down, x)
    for r in range(1, PLANE):
        greet(plane + lax.rem(lane + r, PLANE), x)
    for r in range(1, nx):
        greet(me, lax.rem(x + r, nx))

    def w_part(ref, base, p):
        tall, wide = wr // W_ROW_CUT, depth // W_COL_CUT
        at = base + (p // W_COL_CUT) * tall
        return ref.at[pl.ds(pl.multiple_of(at, 16), tall), pl.ds((p % W_COL_CUT) * wide, wide)]

    own_c = pltpu.make_async_copy(c_ref, cg.at[y, pl.ds(pl.multiple_of(c * WORKB * br, 16), WORKB * br)], own_sem.at[0])
    own_w = pltpu.make_async_copy(w_ref, wg.at[pl.ds(pl.multiple_of(z * wr, 16), wr)], own_sem.at[1])
    own_h = pltpu.make_async_copy(hid_ref, hid, own_sem.at[2])
    own_c.start()
    own_w.start()
    own_h.start()
    pl.semaphore_wait(barrier, 2 + (PLANE - 1) + (nx - 1))

    pending = []

    def go(copy):
        copy.start()
        pending.append(copy)

    def slot_at(yy, cc, h):
        return cg.at[yy, pl.ds(pl.multiple_of((cc * WORKB + h) * br, 16), br)]

    def slot_sem(yy, cc, h):
        return c_recv.at[(yy * NC + cc) * WORKB + h]

    def own_half(h):
        return c_ref.at[pl.ds(h * br, br)]

    parts = W_ROW_CUT * W_COL_CUT
    up_steps = nz // 2
    down_steps = nz - 1 - up_steps

    def w_go(src, zz, p, k, up):
        send = w_send.at[((0 if up else nz) + k) * parts + p]
        go(remote(src, w_part(wg, zz * wr, p), send, w_recv.at[zz * parts + p], z_up if up else z_down, x))

    sends = 0
    for p in range(parts):
        w_go(w_part(w_ref, 0, p), z, p, 0, True)
        w_go(w_part(w_ref, 0, p), z, p, 0, False)
    for h, to in ((0, above), (1, below), (1, above), (0, below), (0, sibling), (1, sibling)):
        go(remote(own_half(h), slot_at(y, c, h), c_send.at[sends], slot_sem(y, c, h), to, x))
        sends += 1

    def row_sums(value):
        lanes = value[:, :128]
        for t in range(1, value.shape[1] // 128):
            lanes = lanes + value[:, t * 128:(t + 1) * 128]
        return jnp.sum(lanes.T, axis=0, keepdims=True)

    own_c.wait()
    own_w.wait()
    own_h.wait()
    h_rows = hid[...].astype(jnp.float32)
    stats[0] = jnp.zeros(stats.shape[1:], jnp.float32)
    stats[0, 0:1, :] = row_sums(h_rows * h_rows)

    def w_step(k):
        for p in range(parts):
            zz = lax.rem(z + nz - k, nz)
            landed(w_part(wg, zz * wr, p), w_recv.at[zz * parts + p])
            if k < up_steps:
                w_go(w_part(wg, zz * wr, p), zz, p, k, True)
            if k <= down_steps:
                zz = lax.rem(z + k, nz)
                landed(w_part(wg, zz * wr, p), w_recv.at[zz * parts + p])
                if k < down_steps:
                    w_go(w_part(wg, zz * wr, p), zz, p, k, False)

    def pass_on(yy, h, to=None):
        nonlocal sends
        landed(slot_at(yy, c, h), slot_sem(yy, c, h))
        for dest in ([] if to is None else [to]) + [sibling]:
            go(remote(slot_at(yy, c, h), slot_at(yy, c, h), c_send.at[sends], slot_sem(yy, c, h), dest, x))
            sends += 1

    def multiply(k, yy):
        for h in range(WORKB):
            landed(slot_at(yy, 1 - c, h), slot_sem(yy, 1 - c, h))

        part = lax.dot_general(wg[...], cg[yy], NT, preferred_element_type=jnp.float32).astype(jnp.bfloat16)
        for xx in range(nx):
            ps[xx, yy] = part[xx * pn:(xx + 1) * pn]

        send_x(k, yy, 0, 0, x2, xl)
        send_x(k, yy, 0, 1, x2, xp)
        send_x(k, yy, 1, 0, xp, xp)
        send_x(k, yy, 1, 1, xl, xl)

    def half_x(half):
        return pl.ds(half * WORKB * br, WORKB * br)

    def send_x(k, yy, kind, half, xx, to):
        i = (k * 3 + kind) * NC + half
        go(remote(
            ps.at[xx, yy, :, half_x(half)], xr.at[kind, yy, :, half_x(half)], x_send.at[i], x_recv.at[i], me, to
        ))

    def wait_x(k, yy, kind, half):
        landed(xr.at[kind, yy, :, half_x(half)], x_recv.at[(k * 3 + kind) * NC + half])

    def relay(k, yy):
        for half, to in ((0, xl), (1, xp)):
            wait_x(k, yy, 0, half)
            own = ps[to, yy, :, half_x(half)].astype(jnp.float32)
            both = own + xr[0, yy, :, half_x(half)].astype(jnp.float32)
            ps[to, yy, :, half_x(half)] = both.astype(jnp.bfloat16)
            send_x(k, yy, 2, half, to, to)

    def combine(k, yy):
        total = ps[x, yy].astype(jnp.float32)
        for kind in (1, 2):
            for half in range(NC):
                wait_x(k, yy, kind, half)
            total = total + xr[kind, yy].astype(jnp.float32)
        total = total.astype(jnp.bfloat16)
        for s in range(NC * WORKB):
            sb[yy, s] = total[:, s * br:(s + 1) * br].reshape(sb.shape[2:])
        for d in range(REACHED):
            dest = dest_of(yy, d)

            @pl.when(dest == me)
            def _():
                pltpu.make_async_copy(*route(yy, d)).start()

            @pl.when(dest != me)
            def _():
                deliver(k, yy, d).start()

    def dest_of(yy, d):
        chip = lax.rem(z * NY + yy - d + nz * NY, nz * NY)
        return chip * NC + c

    def union(d, source):
        count = min(NC * WORKB, SLOTS - d * NC * WORKB)
        return rb.at[pl.ds(d * NC * WORKB, count), :, source]

    def route(yy, d):
        to_ref = union(d, lane)
        return sb.at[yy, pl.ds(0, to_ref.shape[0])], to_ref, s_recv.at[lane * REACHED + d]

    def deliver(k, yy, d):
        from_ref, to_ref, recv = route(yy, d)
        return remote(from_ref, to_ref, s_send.at[k * REACHED + d], recv, dest_of(yy, d), x)

    def share(k):
        for d in range(REACHED):
            source = lax.rem(y + d - STAGES[k] + NY, NY) * NC + c
            at, recv = union(d, source), s_recv.at[source * REACHED + d]
            landed(at, recv)
            go(remote(at, at, s_send.at[(NY + k) * REACHED + d], recv, sibling, x))

    order = [lax.rem(y + step + NY, NY) for step in STAGES]
    for k in range(1, up_steps + 1):
        w_step(k)
        if k == up_steps // 2:
            pass_on(ym, 0, above)
            pass_on(yp, 1, below)
        if k == up_steps - 1:
            pass_on(ym, 1)
            pass_on(yp, 0)
    multiply(0, order[0])
    pass_on(y2, 0)
    pass_on(y2, 1)
    multiply(1, order[1])
    relay(0, order[0])
    multiply(2, order[2])
    relay(1, order[1])
    combine(0, order[0])
    multiply(3, order[3])
    relay(2, order[2])
    combine(1, order[1])
    share(0)
    relay(3, order[3])
    combine(2, order[2])
    share(1)
    combine(3, order[3])
    share(2)
    share(3)

    seq = BLK * br
    target = jnp.where(lax.broadcasted_iota(jnp.int32, (1, seq), 1) < count_ref[0], pos_ref[...], seq)
    place = (lax.broadcasted_iota(jnp.int32, (seq, seq), 0) == target).astype(jnp.float32).astype(jnp.bfloat16)
    for yy in range(NY):
        for d in range(REACHED):
            source = yy * NC + 1 - c
            landed(union(d, source), s_recv.at[source * REACHED + d])
    for b in range(BLK):
        v = slot_ref[0, b]
        block = rb[jnp.maximum(v, 0) + WORKB * c].reshape(rt.shape[0], br)
        rt[:, b * br:(b + 1) * br] = jnp.where(v >= 0, block, jnp.zeros_like(block))
    placed = lax.dot_general(place, rt[...], NT, preferred_element_type=jnp.float32)
    grad_ref[...] = placed.astype(jnp.bfloat16)
    stats[0, 1:2, :] = row_sums(placed * gain_ref[...] * hid[...].astype(jnp.float32))
    for r in range(1, nx):
        go(remote(stats.at[0], stats.at[r], t_send.at[r - 1], t_recv.at[r - 1], me, lax.rem(x + r, nx)))
    total = stats[0]
    for r in range(1, nx):
        landed(stats.at[r], t_recv.at[r - 1])
        total = total + stats[r]
    stat_ref[...] = total

    for copy in pending:
        copy.wait_send()
    for k in range(NY):
        for d in range(REACHED):
            @pl.when(dest_of(order[k], d) != me)
            def _():
                deliver(k, order[k], d).wait_send()


def shards(nz, nx, hidden_in, grad_out, grad_qkv, qkv_weight, norm_gain, image_count, image_pos, block_slot):
    seq, cols = hidden_in.shape
    br = seq // BLK
    depth = grad_qkv.shape[1]
    wr = qkv_weight.shape[0]
    pn = nz * wr // nx
    bf16 = jnp.bfloat16
    dma = pltpu.SemaphoreType.DMA
    vmem = pl.BlockSpec(memory_space=pltpu.VMEM)
    smem = pl.BlockSpec(memory_space=pltpu.SMEM)
    hbm = pl.BlockSpec(memory_space=pl.ANY)
    chip_rows = NC * WORKB * br
    parts = W_ROW_CUT * W_COL_CUT
    head_grad, stats = pl.pallas_call(
        functools.partial(kernel, nz, nx),
        out_shape=(jax.ShapeDtypeStruct((seq, cols), bf16), jax.ShapeDtypeStruct((8, seq), jnp.float32)),
        in_specs=[smem, smem, vmem, vmem, hbm, hbm, hbm],
        out_specs=(vmem, vmem),
        scratch_shapes=[
            pltpu.VMEM((NY, chip_rows, depth), bf16),
            pltpu.VMEM((nz * wr, depth), bf16),
            pltpu.VMEM((nx, NY, pn, chip_rows), bf16),
            pltpu.VMEM((3, NY, pn, chip_rows), bf16),
            pltpu.VMEM((NY, NC * WORKB, nz // nx, wr, br), bf16),
            pltpu.VMEM((SLOTS, nz // nx, PLANE, wr, br), bf16),
            pltpu.VMEM((cols, seq), bf16),
            pltpu.VMEM((seq, cols), bf16),
            pltpu.VMEM((nx, 8, seq), jnp.float32),
            dma((14,)),
            dma((PLANE * WORKB,)),
            dma((2 * nz * parts,)),
            dma((nz * parts,)),
            dma((NY * 3 * NC,)),
            dma((NY * 3 * NC,)),
            dma((2 * NY * REACHED,)),
            dma((PLANE * REACHED,)),
            dma((nx - 1,)),
            dma((nx - 1,)),
            dma((3,)),
        ],
        compiler_params=pltpu.CompilerParams(
            collective_id=0, has_side_effects=True, vmem_limit_bytes=60 * 1024 * 1024
        ),
    )(block_slot, image_count, image_pos[None, :], norm_gain[None, :], hidden_in, grad_qkv, qkv_weight)

    squares, cross = stats[0], stats[1]
    inv_rms = lax.rsqrt(squares / D + 1e-05)
    result = (
        grad_out.astype(jnp.float32)
        + inv_rms[:, None] * (head_grad.astype(jnp.float32) * norm_gain[None, :])
        - hidden_in.astype(jnp.float32) * (inv_rms**3 * cross / D)[:, None]
    )
    return result.astype(bf16)


def solution(mesh):
    nz, nx = mesh.shape["dp"] // PLANE, mesh.shape["mp"]
    return jax.shard_map(
        functools.partial(shards, nz, nx),
        mesh=mesh,
        in_specs=(
            P("dp", "mp"),
            P("dp", "mp"),
            P("dp", "mp"),
            P("dp", "mp"),
            P("mp"),
            P("dp"),
            P("dp"),
            P("dp", None),
        ),
        out_specs=P("dp", "mp"),
        check_vma=False,
    )
```

```python
import functools

import jax
import jax.numpy as jnp
from jax import lax
from jax.experimental import pallas as pl
from jax.experimental.pallas import tpu as pltpu
from jax.sharding import PartitionSpec as P

D = 4096
BLK = 4
REACH = 4
WORKB = 2
NY = 4
NC = 2
PLANE = NY * NC
REACHED = (REACH + NC - 1 + NC - 1) // NC
SLOTS = (REACH + NC - 1) * WORKB
STAGES = (-1, 2, 0, 1)
W_ROW_CUT = 2
W_COL_CUT = 1
MESH = pl.DeviceIdType.MESH
NT = (((1,), (1,)), ((), ()))


def kernel(
    nz, nx, slot_ref, count_ref, pos_ref, gain_ref, hid_ref, go_ref, c_ref, w_ref, out_ref,
    cg, wg, ps, xr, sb, rb, rt, hid, gout, stats,
    c_send, c_recv, w_send, w_recv, x_send, x_recv, s_send, s_recv, t_send, t_recv, own_sem,
):
    br = c_ref.shape[0] // WORKB
    wr, depth = w_ref.shape
    pn = ps.shape[2]
    me = lax.axis_index("dp")
    x = lax.axis_index("mp")
    z, lane = me // PLANE, lax.rem(me, PLANE)
    y, c = lane // NC, lax.rem(lane, NC)
    shards = nz * PLANE
    yp, ym, y2 = lax.rem(y + 1, NY), lax.rem(y + 3, NY), lax.rem(y + 2, NY)
    plane = z * PLANE
    xp, xl, x2 = lax.rem(x + 1, nx), lax.rem(x + nx - 1, nx), lax.rem(x + 2, nx)
    sibling = plane + y * NC + 1 - c
    above, below = plane + yp * NC + c, plane + ym * NC + c
    z_up, z_down = lax.rem(me + PLANE, shards), lax.rem(me + shards - PLANE, shards)

    def remote(src, dst, send, recv, dp_to, x_to):
        return pltpu.make_async_remote_copy(
            src_ref=src, dst_ref=dst, send_sem=send, recv_sem=recv,
            device_id=(dp_to, x_to), device_id_type=MESH,
        )

    def landed(dst, recv):
        remote(dst, dst, own_sem.at[0], recv, sibling, x).wait_recv()

    barrier = pltpu.get_barrier_semaphore()

    def greet(dp_to, x_to):
        pl.semaphore_signal(barrier, inc=1, device_id=(dp_to, x_to), device_id_type=MESH)

    greet(z_up, x)
    greet(z_down, x)
    for r in range(1, PLANE):
        greet(plane + lax.rem(lane + r, PLANE), x)
    for r in range(1, nx):
        greet(me, lax.rem(x + r, nx))

    def w_part(ref, base, p):
        tall, wide = wr // W_ROW_CUT, depth // W_COL_CUT
        at = base + (p // W_COL_CUT) * tall
        return ref.at[pl.ds(pl.multiple_of(at, 16), tall), pl.ds((p % W_COL_CUT) * wide, wide)]

    own_c = pltpu.make_async_copy(c_ref, cg.at[y, pl.ds(pl.multiple_of(c * WORKB * br, 16), WORKB * br)], own_sem.at[0])
    own_w = pltpu.make_async_copy(w_ref, wg.at[pl.ds(pl.multiple_of(z * wr, 16), wr)], own_sem.at[1])
    own_h = pltpu.make_async_copy(hid_ref, hid, own_sem.at[2])
    own_c.start()
    own_w.start()
    own_h.start()
    own_g = pltpu.make_async_copy(go_ref, gout, own_sem.at[3])
    own_g.start()
    pl.semaphore_wait(barrier, 2 + (PLANE - 1) + (nx - 1))

    pending = []

    def go(copy):
        copy.start()
        pending.append(copy)

    def slot_at(yy, cc, h):
        return cg.at[yy, pl.ds(pl.multiple_of((cc * WORKB + h) * br, 16), br)]

    def slot_sem(yy, cc, h):
        return c_recv.at[(yy * NC + cc) * WORKB + h]

    def own_half(h):
        return c_ref.at[pl.ds(h * br, br)]

    parts = W_ROW_CUT * W_COL_CUT
    up_steps = nz // 2
    down_steps = nz - 1 - up_steps

    def w_go(src, zz, p, k, up):
        send = w_send.at[((0 if up else nz) + k) * parts + p]
        go(remote(src, w_part(wg, zz * wr, p), send, w_recv.at[zz * parts + p], z_up if up else z_down, x))

    sends = 0
    for p in range(parts):
        w_go(w_part(w_ref, 0, p), z, p, 0, True)
        w_go(w_part(w_ref, 0, p), z, p, 0, False)
    for h, to in ((0, above), (1, below), (1, above), (0, below), (0, sibling), (1, sibling)):
        go(remote(own_half(h), slot_at(y, c, h), c_send.at[sends], slot_sem(y, c, h), to, x))
        sends += 1

    def row_sums(value):
        lanes = value[:, :128]
        for t in range(1, value.shape[1] // 128):
            lanes = lanes + value[:, t * 128:(t + 1) * 128]
        return jnp.sum(lanes.T, axis=0, keepdims=True)

    own_c.wait()
    own_w.wait()
    own_h.wait()
    h_rows = hid[...].astype(jnp.float32)
    stats[0] = jnp.zeros(stats.shape[1:], jnp.float32)
    stats[0, 0:1, :] = row_sums(h_rows * h_rows)

    def w_step(k):
        for p in range(parts):
            zz = lax.rem(z + nz - k, nz)
            landed(w_part(wg, zz * wr, p), w_recv.at[zz * parts + p])
            if k < up_steps:
                w_go(w_part(wg, zz * wr, p), zz, p, k, True)
            if k <= down_steps:
                zz = lax.rem(z + k, nz)
                landed(w_part(wg, zz * wr, p), w_recv.at[zz * parts + p])
                if k < down_steps:
                    w_go(w_part(wg, zz * wr, p), zz, p, k, False)

    def pass_on(yy, h, to=None):
        nonlocal sends
        landed(slot_at(yy, c, h), slot_sem(yy, c, h))
        for dest in ([] if to is None else [to]) + [sibling]:
            go(remote(slot_at(yy, c, h), slot_at(yy, c, h), c_send.at[sends], slot_sem(yy, c, h), dest, x))
            sends += 1

    def multiply(k, yy):
        for h in range(WORKB):
            landed(slot_at(yy, 1 - c, h), slot_sem(yy, 1 - c, h))

        part = lax.dot_general(wg[...], cg[yy], NT, preferred_element_type=jnp.float32).astype(jnp.bfloat16)
        for xx in range(nx):
            ps[xx, yy] = part[xx * pn:(xx + 1) * pn]

        send_x(k, yy, 0, 0, x2, xl)
        send_x(k, yy, 0, 1, x2, xp)
        send_x(k, yy, 1, 0, xp, xp)
        send_x(k, yy, 1, 1, xl, xl)

    def half_x(half):
        return pl.ds(half * WORKB * br, WORKB * br)

    def send_x(k, yy, kind, half, xx, to):
        i = (k * 3 + kind) * NC + half
        go(remote(
            ps.at[xx, yy, :, half_x(half)], xr.at[kind, yy, :, half_x(half)], x_send.at[i], x_recv.at[i], me, to
        ))

    def wait_x(k, yy, kind, half):
        landed(xr.at[kind, yy, :, half_x(half)], x_recv.at[(k * 3 + kind) * NC + half])

    def relay(k, yy):
        for half, to in ((0, xl), (1, xp)):
            wait_x(k, yy, 0, half)
            own = ps[to, yy, :, half_x(half)].astype(jnp.float32)
            both = own + xr[0, yy, :, half_x(half)].astype(jnp.float32)
            ps[to, yy, :, half_x(half)] = both.astype(jnp.bfloat16)
            send_x(k, yy, 2, half, to, to)

    def combine(k, yy):
        total = ps[x, yy].astype(jnp.float32)
        for kind in (1, 2):
            for half in range(NC):
                wait_x(k, yy, kind, half)
            total = total + xr[kind, yy].astype(jnp.float32)
        total = total.astype(jnp.bfloat16)
        for s in range(NC * WORKB):
            sb[yy, s] = total[:, s * br:(s + 1) * br].reshape(sb.shape[2:])
        for d in range(REACHED):
            dest = dest_of(yy, d)

            @pl.when(dest == me)
            def _():
                pltpu.make_async_copy(*route(yy, d)).start()

            @pl.when(dest != me)
            def _():
                deliver(k, yy, d).start()

    def dest_of(yy, d):
        chip = lax.rem(z * NY + yy - d + nz * NY, nz * NY)
        return chip * NC + c

    def union(d, source):
        count = min(NC * WORKB, SLOTS - d * NC * WORKB)
        return rb.at[pl.ds(d * NC * WORKB, count), :, source]

    def route(yy, d):
        to_ref = union(d, lane)
        return sb.at[yy, pl.ds(0, to_ref.shape[0])], to_ref, s_recv.at[lane * REACHED + d]

    def deliver(k, yy, d):
        from_ref, to_ref, recv = route(yy, d)
        return remote(from_ref, to_ref, s_send.at[k * REACHED + d], recv, dest_of(yy, d), x)

    def share(k):
        for d in range(REACHED):
            source = lax.rem(y + d - STAGES[k] + NY, NY) * NC + c
            at, recv = union(d, source), s_recv.at[source * REACHED + d]
            landed(at, recv)
            go(remote(at, at, s_send.at[(NY + k) * REACHED + d], recv, sibling, x))

    order = [lax.rem(y + step + NY, NY) for step in STAGES]
    for k in range(1, up_steps + 1):
        w_step(k)
        if k == 3:
            pass_on(ym, 0, above)
            pass_on(yp, 1, below)
        if k == up_steps - 1:
            pass_on(ym, 1)
            pass_on(yp, 0)
    multiply(0, order[0])
    pass_on(y2, 0)
    pass_on(y2, 1)
    multiply(1, order[1])
    relay(0, order[0])
    multiply(2, order[2])
    relay(1, order[1])
    combine(0, order[0])
    multiply(3, order[3])
    relay(2, order[2])
    combine(1, order[1])
    share(0)
    relay(3, order[3])
    combine(2, order[2])
    share(1)
    combine(3, order[3])
    share(2)
    share(3)

    seq = BLK * br
    target = jnp.where(lax.broadcasted_iota(jnp.int32, (1, seq), 1) < count_ref[0], pos_ref[...], seq)
    place = (lax.broadcasted_iota(jnp.int32, (seq, seq), 0) == target).astype(jnp.float32).astype(jnp.bfloat16)
    for yy in range(NY):
        for d in range(REACHED):
            source = yy * NC + 1 - c
            landed(union(d, source), s_recv.at[source * REACHED + d])
    for b in range(BLK):
        v = slot_ref[0, b]
        block = rb[jnp.maximum(v, 0) + WORKB * c].reshape(rt.shape[0], br)
        rt[:, b * br:(b + 1) * br] = jnp.where(v >= 0, block, jnp.zeros_like(block))
    placed = lax.dot_general(place, rt[...], NT, preferred_element_type=jnp.float32)
    scaled = placed * gain_ref[...]
    stats[0, 1:2, :] = row_sums(scaled * hid[...].astype(jnp.float32))
    for r in range(1, nx):
        go(remote(stats.at[0], stats.at[r], t_send.at[r - 1], t_recv.at[r - 1], me, lax.rem(x + r, nx)))
    total = stats[0]
    for r in range(1, nx):
        landed(stats.at[r], t_recv.at[r - 1])
        total = total + stats[r]
    own_g.wait()
    inv_rms = lax.rsqrt(total[0:1] / D + 1e-05)
    pull = inv_rms * inv_rms * inv_rms * total[1:2] / D
    inv_rms = jnp.broadcast_to(inv_rms, (128, seq)).T
    pull = jnp.broadcast_to(pull, (128, seq)).T
    for t in range(out_ref.shape[1] // 128):
        at = slice(t * 128, (t + 1) * 128)
        grown = gout[:, at].astype(jnp.float32) + inv_rms * scaled[:, at]
        out_ref[:, at] = (grown - hid[:, at].astype(jnp.float32) * pull).astype(jnp.bfloat16)

    for copy in pending:
        copy.wait_send()
    for k in range(NY):
        for d in range(REACHED):
            @pl.when(dest_of(order[k], d) != me)
            def _():
                deliver(k, order[k], d).wait_send()


def shards(nz, nx, hidden_in, grad_out, grad_qkv, qkv_weight, norm_gain, image_count, image_pos, block_slot):
    seq, cols = hidden_in.shape
    br = seq // BLK
    depth = grad_qkv.shape[1]
    wr = qkv_weight.shape[0]
    pn = nz * wr // nx
    bf16 = jnp.bfloat16
    dma = pltpu.SemaphoreType.DMA
    vmem = pl.BlockSpec(memory_space=pltpu.VMEM)
    smem = pl.BlockSpec(memory_space=pltpu.SMEM)
    hbm = pl.BlockSpec(memory_space=pl.ANY)
    chip_rows = NC * WORKB * br
    parts = W_ROW_CUT * W_COL_CUT
    return pl.pallas_call(
        functools.partial(kernel, nz, nx),
        out_shape=jax.ShapeDtypeStruct((seq, cols), bf16),
        in_specs=[smem, smem, vmem, vmem, hbm, hbm, hbm, hbm],
        out_specs=vmem,
        scratch_shapes=[
            pltpu.VMEM((NY, chip_rows, depth), bf16),
            pltpu.VMEM((nz * wr, depth), bf16),
            pltpu.VMEM((nx, NY, pn, chip_rows), bf16),
            pltpu.VMEM((3, NY, pn, chip_rows), bf16),
            pltpu.VMEM((NY, NC * WORKB, nz // nx, wr, br), bf16),
            pltpu.VMEM((SLOTS, nz // nx, PLANE, wr, br), bf16),
            pltpu.VMEM((cols, seq), bf16),
            pltpu.VMEM((seq, cols), bf16),
            pltpu.VMEM((seq, cols), bf16),
            pltpu.VMEM((nx, 8, seq), jnp.float32),
            dma((14,)),
            dma((PLANE * WORKB,)),
            dma((2 * nz * parts,)),
            dma((nz * parts,)),
            dma((NY * 3 * NC,)),
            dma((NY * 3 * NC,)),
            dma((2 * NY * REACHED,)),
            dma((PLANE * REACHED,)),
            dma((nx - 1,)),
            dma((nx - 1,)),
            dma((4,)),
        ],
        compiler_params=pltpu.CompilerParams(
            collective_id=0, has_side_effects=True, vmem_limit_bytes=60 * 1024 * 1024
        ),
    )(block_slot, image_count, image_pos[None, :], norm_gain[None, :], hidden_in, grad_out, grad_qkv, qkv_weight)


def solution(mesh):
    nz, nx = mesh.shape["dp"] // PLANE, mesh.shape["mp"]
    return jax.shard_map(
        functools.partial(shards, nz, nx),
        mesh=mesh,
        in_specs=(
            P("dp", "mp"),
            P("dp", "mp"),
            P("dp", "mp"),
            P("dp", "mp"),
            P("mp"),
            P("dp"),
            P("dp"),
            P("dp", None),
        ),
        out_specs=P("dp", "mp"),
        check_vma=False,
    )
```

```python
import functools

import jax
import jax.numpy as jnp
from jax import lax
from jax.experimental import pallas as pl
from jax.experimental.pallas import tpu as pltpu
from jax.sharding import PartitionSpec as P

D = 4096
BLK = 4
REACH = 4
WORKB = 2
NY = 4
NC = 2
PLANE = NY * NC
REACHED = (REACH + NC - 1 + NC - 1) // NC
SLOTS = (REACH + NC - 1) * WORKB
STAGES = (-1, 2, 0, 1)
W_ROW_CUT = 2
W_COL_CUT = 1
MESH = pl.DeviceIdType.MESH
NT = (((1,), (1,)), ((), ()))


def kernel(
    nz, nx, slot_ref, count_ref, pos_ref, gain_ref, hid_ref, go_ref, c_ref, w_ref, out_ref,
    cg, wg, ps, xr, sb, rb, rt, hid, gout, stats,
    c_send, c_recv, w_send, w_recv, x_send, x_recv, s_send, s_recv, t_send, t_recv, own_sem,
):
    br = c_ref.shape[0] // WORKB
    wr, depth = w_ref.shape
    pn = ps.shape[2]
    me = lax.axis_index("dp")
    x = lax.axis_index("mp")
    z, lane = me // PLANE, lax.rem(me, PLANE)
    y, c = lane // NC, lax.rem(lane, NC)
    shards = nz * PLANE
    yp, ym, y2 = lax.rem(y + 1, NY), lax.rem(y + 3, NY), lax.rem(y + 2, NY)
    plane = z * PLANE
    xp, xl, x2 = lax.rem(x + 1, nx), lax.rem(x + nx - 1, nx), lax.rem(x + 2, nx)
    sibling = plane + y * NC + 1 - c
    above, below = plane + yp * NC + c, plane + ym * NC + c
    z_up, z_down = lax.rem(me + PLANE, shards), lax.rem(me + shards - PLANE, shards)

    def remote(src, dst, send, recv, dp_to, x_to):
        return pltpu.make_async_remote_copy(
            src_ref=src, dst_ref=dst, send_sem=send, recv_sem=recv,
            device_id=(dp_to, x_to), device_id_type=MESH,
        )

    def landed(dst, recv):
        remote(dst, dst, own_sem.at[0], recv, sibling, x).wait_recv()

    barrier = pltpu.get_barrier_semaphore()

    def greet(dp_to, x_to):
        pl.semaphore_signal(barrier, inc=1, device_id=(dp_to, x_to), device_id_type=MESH)

    greet(z_up, x)
    greet(z_down, x)
    for r in range(1, PLANE):
        greet(plane + lax.rem(lane + r, PLANE), x)
    for r in range(1, nx):
        greet(me, lax.rem(x + r, nx))

    def w_part(ref, base, p):
        tall, wide = wr // W_ROW_CUT, depth // W_COL_CUT
        at = base + (p // W_COL_CUT) * tall
        return ref.at[pl.ds(pl.multiple_of(at, 16), tall), pl.ds((p % W_COL_CUT) * wide, wide)]

    own_c = pltpu.make_async_copy(c_ref, cg.at[y, pl.ds(pl.multiple_of(c * WORKB * br, 16), WORKB * br)], own_sem.at[0])
    own_w = pltpu.make_async_copy(w_ref, wg.at[pl.ds(pl.multiple_of(z * wr, 16), wr)], own_sem.at[1])
    own_h = pltpu.make_async_copy(hid_ref, hid, own_sem.at[2])
    own_c.start()
    own_w.start()
    own_h.start()
    own_g = pltpu.make_async_copy(go_ref, gout, own_sem.at[3])
    own_g.start()
    pl.semaphore_wait(barrier, 2 + (PLANE - 1) + (nx - 1))

    pending = []

    def go(copy):
        copy.start()
        pending.append(copy)

    def drain(count):
        for copy in pending[:count]:
            copy.wait_send()
        del pending[:count]

    def slot_at(yy, cc, h):
        return cg.at[yy, pl.ds(pl.multiple_of((cc * WORKB + h) * br, 16), br)]

    def slot_sem(yy, cc, h):
        return c_recv.at[(yy * NC + cc) * WORKB + h]

    def own_half(h):
        return c_ref.at[pl.ds(h * br, br)]

    parts = W_ROW_CUT * W_COL_CUT
    up_steps = nz // 2
    down_steps = nz - 1 - up_steps

    def w_go(src, zz, p, k, up):
        send = w_send.at[((0 if up else nz) + k) * parts + p]
        go(remote(src, w_part(wg, zz * wr, p), send, w_recv.at[zz * parts + p], z_up if up else z_down, x))

    sends = 0
    for p in range(parts):
        w_go(w_part(w_ref, 0, p), z, p, 0, True)
        w_go(w_part(w_ref, 0, p), z, p, 0, False)
    for h, to in ((0, above), (1, below), (1, above), (0, below), (0, sibling), (1, sibling)):
        go(remote(own_half(h), slot_at(y, c, h), c_send.at[sends], slot_sem(y, c, h), to, x))
        sends += 1

    def row_sums(value):
        lanes = value[:, :128]
        for t in range(1, value.shape[1] // 128):
            lanes = lanes + value[:, t * 128:(t + 1) * 128]
        return jnp.sum(lanes.T, axis=0, keepdims=True)

    own_c.wait()
    own_w.wait()
    own_h.wait()
    h_rows = hid[...].astype(jnp.float32)
    stats[0] = jnp.zeros(stats.shape[1:], jnp.float32)
    stats[0, 0:1, :] = row_sums(h_rows * h_rows)

    def w_step(k):
        for p in range(parts):
            zz = lax.rem(z + nz - k, nz)
            landed(w_part(wg, zz * wr, p), w_recv.at[zz * parts + p])
            if k < up_steps:
                w_go(w_part(wg, zz * wr, p), zz, p, k, True)
            if k <= down_steps:
                zz = lax.rem(z + k, nz)
                landed(w_part(wg, zz * wr, p), w_recv.at[zz * parts + p])
                if k < down_steps:
                    w_go(w_part(wg, zz * wr, p), zz, p, k, False)

    def pass_on(yy, h, to=None):
        nonlocal sends
        landed(slot_at(yy, c, h), slot_sem(yy, c, h))
        for dest in ([] if to is None else [to]) + [sibling]:
            go(remote(slot_at(yy, c, h), slot_at(yy, c, h), c_send.at[sends], slot_sem(yy, c, h), dest, x))
            sends += 1

    def multiply(k, yy):
        for h in range(WORKB):
            landed(slot_at(yy, 1 - c, h), slot_sem(yy, 1 - c, h))

        part = lax.dot_general(wg[...], cg[yy], NT, preferred_element_type=jnp.float32).astype(jnp.bfloat16)
        for xx in range(nx):
            ps[xx, yy] = part[xx * pn:(xx + 1) * pn]

        send_x(k, yy, 0, 0, x2, xl)
        send_x(k, yy, 0, 1, x2, xp)
        send_x(k, yy, 1, 0, xp, xp)
        send_x(k, yy, 1, 1, xl, xl)

    def half_x(half):
        return pl.ds(half * WORKB * br, WORKB * br)

    def send_x(k, yy, kind, half, xx, to):
        i = (k * 3 + kind) * NC + half
        go(remote(
            ps.at[xx, yy, :, half_x(half)], xr.at[kind, yy, :, half_x(half)], x_send.at[i], x_recv.at[i], me, to
        ))

    def wait_x(k, yy, kind, half):
        landed(xr.at[kind, yy, :, half_x(half)], x_recv.at[(k * 3 + kind) * NC + half])

    def relay(k, yy):
        for half, to in ((0, xl), (1, xp)):
            wait_x(k, yy, 0, half)
            own = ps[to, yy, :, half_x(half)].astype(jnp.float32)
            both = own + xr[0, yy, :, half_x(half)].astype(jnp.float32)
            ps[to, yy, :, half_x(half)] = both.astype(jnp.bfloat16)
            send_x(k, yy, 2, half, to, to)

    def combine(k, yy):
        total = ps[x, yy].astype(jnp.float32)
        for kind in (1, 2):
            for half in range(NC):
                wait_x(k, yy, kind, half)
            total = total + xr[kind, yy].astype(jnp.float32)
        total = total.astype(jnp.bfloat16)
        for s in range(NC * WORKB):
            sb[yy, s] = total[:, s * br:(s + 1) * br].reshape(sb.shape[2:])
        for d in range(REACHED):
            dest = dest_of(yy, d)

            @pl.when(dest == me)
            def _():
                pltpu.make_async_copy(*route(yy, d)).start()

            @pl.when(dest != me)
            def _():
                deliver(k, yy, d).start()

    def dest_of(yy, d):
        chip = lax.rem(z * NY + yy - d + nz * NY, nz * NY)
        return chip * NC + c

    def union(d, source):
        count = min(NC * WORKB, SLOTS - d * NC * WORKB)
        return rb.at[pl.ds(d * NC * WORKB, count), :, source]

    def route(yy, d):
        to_ref = union(d, lane)
        return sb.at[yy, pl.ds(0, to_ref.shape[0])], to_ref, s_recv.at[lane * REACHED + d]

    def deliver(k, yy, d):
        from_ref, to_ref, recv = route(yy, d)
        return remote(from_ref, to_ref, s_send.at[k * REACHED + d], recv, dest_of(yy, d), x)

    def share(k):
        for d in range(REACHED):
            source = lax.rem(y + d - STAGES[k] + NY, NY) * NC + c
            at, recv = union(d, source), s_recv.at[source * REACHED + d]
            landed(at, recv)
            go(remote(at, at, s_send.at[(NY + k) * REACHED + d], recv, sibling, x))

    order = [lax.rem(y + step + NY, NY) for step in STAGES]
    for k in range(1, up_steps + 1):
        w_step(k)
        if k == 3:
            pass_on(ym, 0, above)
            pass_on(yp, 1, below)
        if k == up_steps - 1:
            pass_on(ym, 1)
            pass_on(yp, 0)
    gathers = len(pending)
    multiply(0, order[0])
    pass_on(y2, 0)
    pass_on(y2, 1)
    multiply(1, order[1])
    relay(0, order[0])
    multiply(2, order[2])
    relay(1, order[1])
    combine(0, order[0])
    multiply(3, order[3])
    relay(2, order[2])
    combine(1, order[1])
    drain(gathers)
    share(0)
    relay(3, order[3])
    combine(2, order[2])
    share(1)
    combine(3, order[3])
    share(2)
    share(3)

    seq = BLK * br
    target = jnp.where(lax.broadcasted_iota(jnp.int32, (1, seq), 1) < count_ref[...], pos_ref[...], seq)
    place = (lax.broadcasted_iota(jnp.int32, (seq, seq), 0) == target).astype(jnp.float32).astype(jnp.bfloat16)
    for yy in range(NY):
        for d in range(REACHED):
            source = yy * NC + 1 - c
            landed(union(d, source), s_recv.at[source * REACHED + d])
    for b in range(BLK):
        v = slot_ref[0, b]
        block = rb[jnp.maximum(v, 0) + WORKB * c].reshape(rt.shape[0], br)
        rt[:, b * br:(b + 1) * br] = jnp.where(v >= 0, block, jnp.zeros_like(block))
    placed = lax.dot_general(place, rt[...], NT, preferred_element_type=jnp.float32)
    scaled = placed * gain_ref[...]
    stats[0, 1:2, :] = row_sums(scaled * hid[...].astype(jnp.float32))
    for r in range(1, nx):
        go(remote(stats.at[0], stats.at[r], t_send.at[r - 1], t_recv.at[r - 1], me, lax.rem(x + r, nx)))
    drain(len(pending) - 3)
    for k in range(NY):
        for d in range(REACHED):
            @pl.when(dest_of(order[k], d) != me)
            def _():
                deliver(k, order[k], d).wait_send()
    total = stats[0]
    for r in range(1, nx):
        landed(stats.at[r], t_recv.at[r - 1])
        total = total + stats[r]
    own_g.wait()
    inv_rms = lax.rsqrt(total[0:1] / D + 1e-05)
    pull = inv_rms * inv_rms * inv_rms * total[1:2] / D
    inv_rms = jnp.broadcast_to(inv_rms, (128, seq)).T
    pull = jnp.broadcast_to(pull, (128, seq)).T
    for t in range(out_ref.shape[1] // 128):
        at = slice(t * 128, (t + 1) * 128)
        grown = gout[:, at].astype(jnp.float32) + inv_rms * scaled[:, at]
        out_ref[:, at] = (grown - hid[:, at].astype(jnp.float32) * pull).astype(jnp.bfloat16)
    drain(3)


def shards(nz, nx, hidden_in, grad_out, grad_qkv, qkv_weight, norm_gain, image_count, image_pos, block_slot):
    seq, cols = hidden_in.shape
    br = seq // BLK
    depth = grad_qkv.shape[1]
    wr = qkv_weight.shape[0]
    pn = nz * wr // nx
    bf16 = jnp.bfloat16
    dma = pltpu.SemaphoreType.DMA
    vmem = pl.BlockSpec(memory_space=pltpu.VMEM)
    smem = pl.BlockSpec(memory_space=pltpu.SMEM)
    hbm = pl.BlockSpec(memory_space=pl.ANY)
    chip_rows = NC * WORKB * br
    parts = W_ROW_CUT * W_COL_CUT
    return pl.pallas_call(
        functools.partial(kernel, nz, nx),
        out_shape=jax.ShapeDtypeStruct((seq, cols), bf16),
        in_specs=[smem, vmem, vmem, vmem, hbm, hbm, hbm, hbm],
        out_specs=vmem,
        scratch_shapes=[
            pltpu.VMEM((NY, chip_rows, depth), bf16),
            pltpu.VMEM((nz * wr, depth), bf16),
            pltpu.VMEM((nx, NY, pn, chip_rows), bf16),
            pltpu.VMEM((3, NY, pn, chip_rows), bf16),
            pltpu.VMEM((NY, NC * WORKB, nz // nx, wr, br), bf16),
            pltpu.VMEM((SLOTS, nz // nx, PLANE, wr, br), bf16),
            pltpu.VMEM((cols, seq), bf16),
            pltpu.VMEM((seq, cols), bf16),
            pltpu.VMEM((seq, cols), bf16),
            pltpu.VMEM((nx, 8, seq), jnp.float32),
            dma((14,)),
            dma((PLANE * WORKB,)),
            dma((2 * nz * parts,)),
            dma((nz * parts,)),
            dma((NY * 3 * NC,)),
            dma((NY * 3 * NC,)),
            dma((2 * NY * REACHED,)),
            dma((PLANE * REACHED,)),
            dma((nx - 1,)),
            dma((nx - 1,)),
            dma((4,)),
        ],
        compiler_params=pltpu.CompilerParams(
            collective_id=0, has_side_effects=True, vmem_limit_bytes=60 * 1024 * 1024
        ),
    )(block_slot, image_count[None, :], image_pos[None, :], norm_gain[None, :], hidden_in, grad_out, grad_qkv, qkv_weight)


def solution(mesh):
    nz, nx = mesh.shape["dp"] // PLANE, mesh.shape["mp"]
    return jax.shard_map(
        functools.partial(shards, nz, nx),
        mesh=mesh,
        in_specs=(
            P("dp", "mp"),
            P("dp", "mp"),
            P("dp", "mp"),
            P("dp", "mp"),
            P("mp"),
            P("dp"),
            P("dp"),
            P("dp", None),
        ),
        out_specs=P("dp", "mp"),
        check_vma=False,
    )
```
